32 devices in a mesh: redist: 16 (over z, y, x), rep: 2 (over core).
Axes of the slice: x: 2, y: 2, z: 4, core: 2. Of those that a mesh axis runs over, the one named last changes fastest.
Arguments:
- amplitudes: float32 [8, 256, 2, 3840], P(None, 'redist', 'rep'), may hold values from -6 to 6
- integrals: float32 [16, 7680, 2, 1920], P('redist', None, 'rep'), may hold values from -0.0625 to 0.0625
- pair_count: int32 [8], replicated, may hold values from 5760 to 7680, as said below
Outputs:
- cycle_term: float32 [8, 256, 2, 3840], P(None, 'redist', 'rep')
The draws below stay inside these ranges and needn't reach their ends.
Inputs may be any that keep to these rules, and one draw needn't show every extreme that they name: `pair_count`: each block has at least 5760 live pair slots; some block has all 7680 live.
All inputs are finite; a program needn't handle non-finite values.
Results may differ from the reference program's by a relative error of at most 0.00007.
Values sent between devices are 32-bit elements; how exact they have to be, the bound alone decides.
A program may use at most 128 MiB of HBM per device.

```python
import jax
import jax.numpy as jnp
from jax import lax

NBLK = 8
HP = 3840
RB = 256
PCAP = 7680
KSPLIT = 2
JSPLIT = 1
JW = 7680
KW = 1920


def draw_pair_count(key, part):
    key_base, key_pick = jax.random.split(jax.random.fold_in(key, 17))
    count_base = jax.random.randint(key_base, (NBLK,), PCAP * 3 // 4, PCAP + 1)
    chosen = jax.random.randint(key_pick, (), 0, NBLK)
    return jnp.where(lax.iota(jnp.int32, NBLK) == chosen, PCAP, count_base).astype(jnp.int32)


def levels(own_key, shape, shards, least, largest):
    factor_of = 1.0
    for position, shards_of in shards:
        steps = jax.random.uniform(jax.random.fold_in(jax.random.fold_in(own_key, 6), position), (shards_of,), jnp.float32, least / len(shards), largest / len(shards))
        factor_of = factor_of * jnp.repeat(jnp.exp(steps), shape[position] // shards_of).reshape((-1,) + (1,) * (len(shape) - 1 - position))
    return factor_of


def normal_values(rng, dims, scale, reach, shards=(), kind=jnp.bfloat16):
    level = levels(rng, dims, shards, -0.22, 0.18) if shards else 1.0
    entries = jax.random.normal(rng, dims, jnp.float32) * scale * level
    return jnp.minimum(jnp.maximum(entries, -reach), reach).astype(kind)


def setup_inputs(seed: int = 0) -> dict:
    seeds = jax.random.split(jax.random.key(seed), 4)
    amplitudes = normal_values(seeds[0], (NBLK, RB, 2, HP), 1.0, 6.0, ((1, 16), (2, 2)), jnp.float32)
    integrals = normal_values(seeds[1], (NBLK * JSPLIT * KSPLIT, JW, 2, KW), PCAP ** -0.5, 0.0625, ((0, 16), (2, 2)), jnp.float32)
    pair_count = draw_pair_count(jax.random.fold_in(seeds[3], 71), 0)
    return dict(amplitudes=amplitudes, integrals=integrals, pair_count=pair_count)


def reference(amplitudes, integrals, pair_count):
    pair_slots = 2 * HP
    slot_index = lax.iota(jnp.int32, pair_slots)
    live_mask = (slot_index[None, :] < pair_count[:, None]).astype(jnp.float32)
    masked_amp = amplitudes.reshape(NBLK, RB, pair_slots) * live_mask[:, None, :]
    tiles = integrals.reshape(NBLK, JSPLIT, KSPLIT, JW, 2, KW)

    def one_block(operands):
        block_amp, block_tiles, block_mask = operands
        weight = block_tiles.transpose(0, 2, 3, 1, 4).reshape(pair_slots, pair_slots)
        product = lax.dot_general(block_amp, weight, (((1,), (1,)), ((), ())), precision=lax.Precision.HIGHEST, preferred_element_type=jnp.float32)
        return product * block_mask[None, :]

    cycle_term = lax.map(one_block, (masked_amp, tiles, live_mask))
    return cycle_term.reshape(NBLK, RB, 2, HP)
```

```python
import functools

import jax
import jax.numpy as jnp
from jax import lax
from jax.experimental import pallas as pl
from jax.experimental.pallas import tpu as pltpu
from jax.sharding import PartitionSpec as P

NBLK = 8
LANES = 128
CHUNK = 256
MESH = pl.DeviceIdType.MESH


def arrange(moved, rows, jb_split, kc_split, col_width, half_slots):
    summed = moved.reshape(NBLK, jb_split, kc_split, rows, col_width).sum(axis=2)
    return summed.transpose(0, 2, 1, 3).reshape(NBLK, rows, 2, half_slots)


def contract_and_reduce(
    amp, tiles, out,
    a_in, a_parts, w_in, w_hi0, w_lo0, w_hi1, w_lo1, rep_out, rep_in, own, x_out, keep, x_in, final,
    a_send, a_recv, a_local, w_sem, rep_send, rep_recv, x_send, x_recv, o_send, o_recv, o_local,
):
    n = 2 * NBLK
    rows, half = amp.shape[1], amp.shape[2]
    width = half // 2
    pieces = width // LANES
    total = n * rows
    part = NBLK * rows
    chunks = half // CHUNK
    me, core = lax.axis_index("redist"), lax.axis_index("rep")
    block, mine = me // 2, me % 2
    place = mine * NBLK + block

    def w_copy(t, slot, which):
        h = 1 - core if which == 0 else core
        first = pl.multiple_of((h * half + t * CHUNK) * pieces, 8)
        return pltpu.make_async_copy(
            tiles.at[pl.ds(first, CHUNK * pieces), :], w_in.at[slot, which], w_sem.at[slot, which]
        )

    def a_piece(tile):
        return amp.at[tile // 2, :, pl.ds(pl.multiple_of((tile % 2) * width, LANES), width)]

    def a_copy(tile):
        return pltpu.make_async_remote_copy(
            src_ref=a_piece(tile), dst_ref=a_in.at[place],
            send_sem=a_send.at[tile], recv_sem=a_recv.at[place],
            device_id=(tile, core), device_id_type=MESH,
        )

    def a_arrival(source):
        return pltpu.make_async_remote_copy(
            src_ref=a_piece(source), dst_ref=a_in.at[source % 2 * NBLK + source // 2],
            send_sem=a_send.at[source], recv_sem=a_recv.at[source % 2 * NBLK + source // 2],
            device_id=(source, core), device_id_type=MESH,
        )

    def far(i):
        return (1 - me // NBLK) * NBLK + (me + i) % NBLK

    def near(i):
        return me // NBLK * NBLK + (me + i) % NBLK

    for which in range(2):
        w_copy(0, 0, which).start()
    local = pltpu.make_async_copy(a_piece(me), a_in.at[place], a_local)
    local.start()

    barrier = pltpu.get_barrier_semaphore()
    pl.semaphore_signal(barrier, inc=1, device_id=(me, 1 - core), device_id_type=MESH)

    @pl.loop(1, n)
    def _(i):
        pl.semaphore_signal(barrier, inc=1, device_id=((me + i) % n, core), device_id_type=MESH)

    pl.semaphore_wait(barrier, n)

    @pl.loop(0, NBLK)
    def _(i):
        a_copy(far(i)).start()

    @pl.loop(1, NBLK)
    def _(i):
        a_copy(near(i)).start()

    def split_rows(at):
        first = pl.multiple_of(at * rows, rows)
        value = a_in[at]
        high = value.astype(jnp.bfloat16)
        a_parts[pl.ds(first, rows), :] = high
        a_parts[pl.ds(total + first, rows), :] = (value - high.astype(jnp.float32)).astype(jnp.bfloat16)

    local.wait()
    split_rows(place)

    @pl.loop(1, NBLK)
    def _(i):
        source = near(i)
        a_arrival(source).wait_recv()
        split_rows(source % 2 * NBLK + source // 2)

    @pl.loop(0, NBLK)
    def _(i):
        source = far(i)
        a_arrival(source).wait_recv()
        split_rows(source % 2 * NBLK + source // 2)

    def rep_copy(t):
        return pltpu.make_async_remote_copy(
            src_ref=rep_out.at[t], dst_ref=rep_in.at[t],
            send_sem=rep_send.at[t], recv_sem=rep_recv.at[t],
            device_id=(me, 1 - core), device_id_type=MESH,
        )

    def x_copy(t):
        return pltpu.make_async_remote_copy(
            src_ref=x_out.at[t], dst_ref=x_in.at[t],
            send_sem=x_send.at[t], recv_sem=x_recv.at[t],
            device_id=(block * 2 + 1 - mine, core), device_id_type=MESH,
        )

    def o_dst(t):
        return out.at[block, :, pl.ds(pl.multiple_of(t * CHUNK, CHUNK), CHUNK)]

    def o_src(t, owner):
        return final.at[t, pl.ds(pl.multiple_of(owner * rows, rows), rows), :]

    def o_copy(t, owner):
        return pltpu.make_async_remote_copy(
            src_ref=o_src(t, owner), dst_ref=o_dst(t),
            send_sem=o_send.at[owner], recv_sem=o_recv.at[block],
            device_id=(owner * 2 + mine, core), device_id_type=MESH,
        )

    contract = functools.partial(
        lax.dot_general, dimension_numbers=(((1,), (1,)), ((), ())), preferred_element_type=jnp.float32
    )

    def product(slot, which, w_hi, w_lo):
        source = w_in.at[slot, which]
        for c in range(pieces):
            at = slice(c * LANES, (c + 1) * LANES)
            value = source[pl.ds(c, CHUNK, stride=pieces), :]
            high = value.astype(jnp.bfloat16)
            w_hi[:, at] = high
            w_lo[:, at] = (value - high.astype(jnp.float32)).astype(jnp.bfloat16)
        first = contract(a_parts[...], w_hi[...])
        second = contract(a_parts[:total, :], w_lo[...])
        return first[:total] + (first[total:] + second)

    def multiply(t):
        slot = t % 2

        @pl.when(t + 1 < chunks)
        def _():
            w_copy(t + 1, 1 - slot, 0).start()
            w_copy(t + 1, 1 - slot, 1).start()

        w_copy(t, slot, 0).wait()
        rep_out[t] = product(slot, 0, w_hi0, w_lo0)
        rep_copy(t).start()
        w_copy(t, slot, 1).wait()
        own[slot] = product(slot, 1, w_hi1, w_lo1)

    def sum_cores(t):
        slot = t % 2
        rep_copy(t).wait_recv()
        there = pl.ds(pl.multiple_of((1 - mine) * part, part), part)
        here = pl.ds(pl.multiple_of(mine * part, part), part)
        x_out[t] = own[slot, there, :] + rep_in[t, there, :]
        x_copy(t).start()
        keep[t % 4] = own[slot, here, :] + rep_in[t, here, :]

    def sum_pieces(t):
        x_copy(t).wait_recv()
        final[t] = keep[t % 4] + x_in[t]

        @pl.loop(0, NBLK // 2)
        def _(i):
            o_copy(t, (1 - block // 4) * 4 + (block + i) % 4).start()

        @pl.loop(1, NBLK // 2)
        def _(i):
            o_copy(t, block // 4 * 4 + (block + i) % 4).start()

        pltpu.make_async_copy(o_src(t, block), o_dst(t), o_local).start()

    @pl.loop(0, chunks + 3)
    def _(t):
        @pl.when((t >= 1) & (t < chunks + 1))
        def _():
            sum_cores(t - 1)

        @pl.when(t < chunks)
        def _():
            multiply(t)

        @pl.when(t >= 3)
        def _():
            sum_pieces(t - 3)

    @pl.loop(0, chunks)
    def _(t):
        rep_copy(t).wait_send()
        x_copy(t).wait_send()

    @pl.loop(1, n)
    def _(i):
        a_copy((me + i) % n).wait_send()

    pltpu.make_async_copy(out.at[block], out.at[block], o_local).wait()

    @pl.loop(1, NBLK)
    def _(i):
        owner = (block + i) % NBLK
        pltpu.make_async_remote_copy(
            src_ref=out.at[owner], dst_ref=out.at[owner],
            send_sem=o_send.at[owner], recv_sem=o_recv.at[owner],
            device_id=(owner * 2 + mine, core), device_id_type=MESH,
        ).wait()


def fused(masked, tiles):
    rows, half = masked.shape[1], masked.shape[2]
    width = half // 2
    total, part, chunks = 2 * NBLK * rows, NBLK * rows, half // CHUNK
    f32, bf16, dma = jnp.float32, jnp.bfloat16, pltpu.SemaphoreType.DMA
    return pl.pallas_call(
        contract_and_reduce,
        out_shape=jax.ShapeDtypeStruct(masked.shape, f32),
        in_specs=[pl.BlockSpec(memory_space=pl.ANY)] * 2,
        out_specs=pl.BlockSpec(memory_space=pl.ANY),
        scratch_shapes=[
            pltpu.VMEM((2 * NBLK, rows, width), f32),
            pltpu.VMEM((2 * total, width), bf16),
            pltpu.VMEM((2, 2, CHUNK * width // LANES, LANES), f32),
            pltpu.VMEM((CHUNK, width), bf16),
            pltpu.VMEM((CHUNK, width), bf16),
            pltpu.VMEM((CHUNK, width), bf16),
            pltpu.VMEM((CHUNK, width), bf16),
            pltpu.VMEM((chunks, total, CHUNK), f32),
            pltpu.VMEM((chunks, total, CHUNK), f32),
            pltpu.VMEM((2, total, CHUNK), f32),
            pltpu.VMEM((chunks, part, CHUNK), f32),
            pltpu.VMEM((4, part, CHUNK), f32),
            pltpu.VMEM((chunks, part, CHUNK), f32),
            pltpu.VMEM((chunks, part, CHUNK), f32),
            dma((2 * NBLK,)), dma((2 * NBLK,)), dma,
            dma((2, 2)),
            dma((chunks,)), dma((chunks,)),
            dma((chunks,)), dma((chunks,)),
            dma((NBLK,)), dma((NBLK,)), dma,
        ],
        compiler_params=pltpu.CompilerParams(
            collective_id=0, has_side_effects=True, vmem_limit_bytes=50 * 1024 * 1024
        ),
        cost_estimate=pl.CostEstimate(
            flops=6 * total * width * 2 * half, bytes_accessed=tiles.size * 4, transcendentals=0
        ),
    )(masked, tiles)


def on_device(amplitudes, integrals, pair_count):
    half_slots = amplitudes.shape[3]
    row_count = amplitudes.shape[1]
    col_width = integrals.shape[1]
    kc_width = integrals.shape[3]
    kc_split = half_slots // kc_width
    jb_split = 2 * half_slots // col_width
    device_count = lax.axis_size("redist")
    half_index = lax.axis_index("rep")
    slot_index = half_index * half_slots + lax.iota(jnp.int32, half_slots)
    live_mask = (slot_index[None, :] < pair_count[:, None]).astype(jnp.float32)
    masked = amplitudes[:, :, 0, :] * live_mask[:, None, :]
    if (
        jb_split == 1 and kc_split == 2 and device_count == 2 * NBLK
        and row_count % 16 == 0 and half_slots % CHUNK == 0 and kc_width % LANES == 0
    ):
        result = fused(masked, integrals.reshape(-1, LANES))
        return (result * live_mask[:, None, :])[:, :, None, :]
    pieces = masked.reshape(NBLK, row_count, kc_split, kc_width).transpose(0, 2, 1, 3)
    outgoing = jnp.broadcast_to(
        pieces[:, None], (NBLK, jb_split, kc_split, row_count, kc_width)
    ).reshape(device_count, row_count, kc_width)
    tile_matrix = integrals[0, :, 0, :]
    partial_value = jnp.einsum(
        "srk,jk->srj",
        lax.all_to_all(outgoing, "redist", split_axis=0, concat_axis=0, tiled=True),
        tile_matrix,
        precision=lax.Precision.HIGHEST,
        preferred_element_type=jnp.float32,
    )
    moved = lax.all_to_all(partial_value, "redist", split_axis=0, concat_axis=0, tiled=True)
    arranged = arrange(moved, row_count, jb_split, kc_split, col_width, half_slots)
    result = lax.psum_scatter(arranged, "rep", scatter_dimension=2, tiled=True)
    return result * live_mask[:, None, None, :]


def solution(mesh):
    placed = (P(None, "redist", "rep", None), P("redist", None, "rep", None), P())
    return jax.shard_map(
        on_device,
        mesh=mesh,
        in_specs=placed,
        out_specs=P(None, "redist", "rep", None),
        check_vma=False,
    )
```

```python
import jax
import jax.numpy as jnp
from jax import lax
from jax.experimental import pallas as pl
from jax.experimental.pallas import tpu as pltpu
from jax.sharding import PartitionSpec as P

NBLK = 8
LANES = 128
CHUNK = 256
MESH = pl.DeviceIdType.MESH


def arrange(moved, rows, jb_split, kc_split, col_width, half_slots):
    summed = moved.reshape(NBLK, jb_split, kc_split, rows, col_width).sum(axis=2)
    return summed.transpose(0, 2, 1, 3).reshape(NBLK, rows, 2, half_slots)


def contract_and_reduce(
    amp, tiles, out,
    a_in, a_parts, w_in, w_kept, w_now0, w_now1, rep_out, rep_in, own, x_out, keep, x_in, final,
    a_send, a_recv, a_local, w_sem, rep_send, rep_recv, x_send, x_recv, o_send, o_recv, o_local,
):
    n = 2 * NBLK
    zone = NBLK // 2
    rows, half = amp.shape[1], amp.shape[2]
    width = half // 2
    pieces = width // LANES
    part = NBLK * rows
    chunks = half // CHUNK
    kept = w_kept.shape[0]
    me, core = lax.axis_index("redist"), lax.axis_index("rep")
    block, mine = me // 2, me % 2

    def position(owner):
        return (owner // NBLK + me // NBLK) % 2 * NBLK + owner % 2 * zone + owner // 2 % zone

    def w_copy(u, which):
        h = 1 - core if which == 0 else core
        t = jnp.where(u < chunks, u, u - (chunks - kept))
        first = pl.multiple_of((h * half + t * CHUNK) * pieces, 8)
        return pltpu.make_async_copy(
            tiles.at[pl.ds(first, CHUNK * pieces), :], w_in.at[u % 2, which], w_sem.at[u % 2, which]
        )

    def a_piece(tile):
        return amp.at[tile // 2, :, pl.ds(pl.multiple_of((tile % 2) * width, LANES), width)]

    def a_slot(at):
        return a_in.at[pl.ds(pl.multiple_of(at * rows, rows), rows), :]

    def a_copy(tile):
        at = (tile // NBLK + me // NBLK) % 2 * NBLK + mine * zone + block % zone
        return pltpu.make_async_remote_copy(
            src_ref=a_piece(tile), dst_ref=a_slot(at),
            send_sem=a_send.at[tile], recv_sem=a_recv.at[at],
            device_id=(tile, core), device_id_type=MESH,
        )

    def a_arrival(source):
        return pltpu.make_async_remote_copy(
            src_ref=a_piece(source), dst_ref=a_slot(position(source)),
            send_sem=a_send.at[source], recv_sem=a_recv.at[position(source)],
            device_id=(source, core), device_id_type=MESH,
        )

    def far(i):
        return (1 - me // NBLK) * NBLK + (me + i) % NBLK

    def near(i):
        return me // NBLK * NBLK + (me + i) % NBLK

    w_copy(0, 0).start()
    w_copy(0, 1).start()
    local = pltpu.make_async_copy(a_piece(me), a_slot(position(me)), a_local)
    local.start()

    barrier = pltpu.get_barrier_semaphore()
    pl.semaphore_signal(barrier, inc=1, device_id=(me, 1 - core), device_id_type=MESH)

    @pl.loop(1, n)
    def _(i):
        pl.semaphore_signal(barrier, inc=1, device_id=((me + i) % n, core), device_id_type=MESH)

    pl.semaphore_wait(barrier, n)

    @pl.loop(1, NBLK)
    def _(i):
        a_copy(near(i)).start()
        a_copy(far(i)).start()

    a_copy(far(0)).start()

    def split(u, which, w_parts):
        w_copy(u, which).wait()
        source = w_in.at[u % 2, which]
        for c in range(pieces):
            at = slice(c * LANES, (c + 1) * LANES)
            value = source[pl.ds(c, CHUNK, stride=pieces), :]
            high = value.astype(jnp.bfloat16)
            w_parts[:CHUNK, at] = high
            w_parts[CHUNK:, at] = (value - high.astype(jnp.float32)).astype(jnp.bfloat16)

    def fetch(u):
        w_copy(u, 0).start()
        w_copy(u, 1).start()

    @pl.loop(0, kept)
    def _(t):
        fetch(t + 1)
        split(t, 0, w_kept.at[t, 0])
        split(t, 1, w_kept.at[t, 1])

    def split_rows(group):
        for c in range(pieces):
            at = slice(c * LANES, (c + 1) * LANES)
            value = a_in[group * part:(group + 1) * part, at].T
            high = value.astype(jnp.bfloat16)
            a_parts[group, at, :part] = high
            a_parts[group, at, part:] = (value - high.astype(jnp.float32)).astype(jnp.bfloat16)

    def rep_copy(q):
        return pltpu.make_async_remote_copy(
            src_ref=rep_out.at[q], dst_ref=rep_in.at[q],
            send_sem=rep_send.at[q], recv_sem=rep_recv.at[q],
            device_id=(me, 1 - core), device_id_type=MESH,
        )

    def x_copy(q):
        return pltpu.make_async_remote_copy(
            src_ref=x_out.at[q], dst_ref=x_in.at[q],
            send_sem=x_send.at[q], recv_sem=x_recv.at[q],
            device_id=(block * 2 + 1 - mine, core), device_id_type=MESH,
        )

    def o_dst(q):
        return out.at[block, :, pl.ds(pl.multiple_of(q % chunks * CHUNK, CHUNK), CHUNK)]

    def o_src(q, owner):
        return final.at[q, pl.ds(pl.multiple_of(owner % zone * rows, rows), rows), :]

    def o_copy(q, owner):
        return pltpu.make_async_remote_copy(
            src_ref=o_src(q, owner), dst_ref=o_dst(q),
            send_sem=o_send.at[owner], recv_sem=o_recv.at[block],
            device_id=(owner * 2 + mine, core), device_id_type=MESH,
        )

    def product(w_parts, group):
        value = jnp.dot(w_parts[...], a_parts[group], preferred_element_type=jnp.float32)
        high = value[:CHUNK, :part]
        low = value[CHUNK:, :part] + value[:CHUNK, part:]
        return high + (low + value[CHUNK:, part:])

    def sum_cores(q):
        value = (own[q % 2] + rep_in[q]).T
        first, second = value[:part // 2], value[part // 2:]
        x_out[q] = jnp.where(mine == 0, second, first)
        x_copy(q).start()
        keep[q % 4] = jnp.where(mine == 0, first, second)

    def sum_pieces(q):
        x_copy(q).wait_recv()
        final[q] = keep[q % 4] + x_in[q]
        group = q // chunks
        side = (block // zone + group) % 2 * zone

        @pl.when(group == 0)
        def _():
            pltpu.make_async_copy(o_src(q, block), o_dst(q), o_local).start()

        @pl.when(group == 1)
        def _():
            o_copy(q, side + block % zone).start()

        @pl.loop(1, zone)
        def _(i):
            o_copy(q, side + (block + i) % zone).start()

    def settle(q):
        @pl.when(q >= 1)
        def _():
            rep_copy(q - 1).wait_recv()
            sum_cores(q - 1)

    def deliver(q):
        @pl.when(q >= 3)
        def _():
            sum_pieces(q - 3)

    def work(group):
        @pl.loop(group * chunks, group * chunks + kept)
        def _(q):
            settle(q)
            t = q - group * chunks
            rep_out[q] = product(w_kept.at[t, 0], group)
            rep_copy(q).start()
            own[q % 2] = product(w_kept.at[t, 1], group)
            deliver(q)

        @pl.loop(group * chunks + kept, (group + 1) * chunks)
        def _(q):
            settle(q)
            u = q - group * kept

            @pl.when(u + 1 < 2 * chunks - kept)
            def _():
                fetch(u + 1)

            split(u, 0, w_now0)
            rep_out[q] = product(w_now0, group)
            rep_copy(q).start()
            split(u, 1, w_now1)
            own[q % 2] = product(w_now1, group)
            deliver(q)

    local.wait()

    @pl.loop(1, NBLK)
    def _(i):
        a_arrival(near(i)).wait_recv()

    split_rows(0)
    work(0)

    @pl.loop(0, NBLK)
    def _(i):
        a_arrival(far(i)).wait_recv()

    split_rows(1)
    work(1)

    steps = 2 * chunks
    rep_copy(steps - 1).wait_recv()
    sum_cores(steps - 1)

    @pl.loop(steps - 3, steps)
    def _(q):
        sum_pieces(q)

    @pl.loop(0, steps)
    def _(q):
        rep_copy(q).wait_send()
        x_copy(q).wait_send()

    @pl.loop(1, n)
    def _(i):
        a_copy((me + i) % n).wait_send()

    pltpu.make_async_copy(out.at[block], out.at[block], o_local).wait()

    @pl.loop(1, NBLK)
    def _(i):
        owner = (block + i) % NBLK
        pltpu.make_async_remote_copy(
            src_ref=out.at[owner], dst_ref=out.at[owner],
            send_sem=o_send.at[owner], recv_sem=o_recv.at[owner],
            device_id=(owner * 2 + mine, core), device_id_type=MESH,
        ).wait()


def fused(masked, tiles):
    rows, half = masked.shape[1], masked.shape[2]
    width = half // 2
    total, part, chunks = 2 * NBLK * rows, NBLK * rows, half // CHUNK
    kept, steps = chunks // 2, 2 * chunks
    f32, bf16, dma = jnp.float32, jnp.bfloat16, pltpu.SemaphoreType.DMA
    return pl.pallas_call(
        contract_and_reduce,
        out_shape=jax.ShapeDtypeStruct(masked.shape, f32),
        in_specs=[pl.BlockSpec(memory_space=pl.ANY)] * 2,
        out_specs=pl.BlockSpec(memory_space=pl.ANY),
        scratch_shapes=[
            pltpu.VMEM((total, width), f32),
            pltpu.VMEM((2, width, 2 * part), bf16),
            pltpu.VMEM((2, 2, CHUNK * width // LANES, LANES), f32),
            pltpu.VMEM((kept, 2, 2 * CHUNK, width), bf16),
            pltpu.VMEM((2 * CHUNK, width), bf16),
            pltpu.VMEM((2 * CHUNK, width), bf16),
            pltpu.VMEM((steps, CHUNK, part), f32),
            pltpu.VMEM((steps, CHUNK, part), f32),
            pltpu.VMEM((2, CHUNK, part), f32),
            pltpu.VMEM((steps, part // 2, CHUNK), f32),
            pltpu.VMEM((4, part // 2, CHUNK), f32),
            pltpu.VMEM((steps, part // 2, CHUNK), f32),
            pltpu.VMEM((steps, part // 2, CHUNK), f32),
            dma((2 * NBLK,)), dma((2 * NBLK,)), dma,
            dma((2, 2)),
            dma((steps,)), dma((steps,)),
            dma((steps,)), dma((steps,)),
            dma((NBLK,)), dma((NBLK,)), dma,
        ],
        compiler_params=pltpu.CompilerParams(
            collective_id=0, has_side_effects=True, vmem_limit_bytes=60 * 1024 * 1024
        ),
        cost_estimate=pl.CostEstimate(
            flops=8 * total * width * 2 * half, bytes_accessed=tiles.size * 6, transcendentals=0
        ),
    )(masked, tiles)


def on_device(amplitudes, integrals, pair_count):
    half_slots = amplitudes.shape[3]
    row_count = amplitudes.shape[1]
    col_width = integrals.shape[1]
    kc_width = integrals.shape[3]
    kc_split = half_slots // kc_width
    jb_split = 2 * half_slots // col_width
    device_count = lax.axis_size("redist")
    half_index = lax.axis_index("rep")
    slot_index = half_index * half_slots + lax.iota(jnp.int32, half_slots)
    live_mask = (slot_index[None, :] < pair_count[:, None]).astype(jnp.float32)
    masked = amplitudes[:, :, 0, :] * live_mask[:, None, :]
    if (
        jb_split == 1 and kc_split == 2 and device_count == 2 * NBLK
        and row_count * NBLK == LANES and half_slots % CHUNK == 0 and kc_width % LANES == 0
    ):
        result = fused(masked, integrals.reshape(-1, LANES))
        return (result * live_mask[:, None, :])[:, :, None, :]
    pieces = masked.reshape(NBLK, row_count, kc_split, kc_width).transpose(0, 2, 1, 3)
    outgoing = jnp.broadcast_to(
        pieces[:, None], (NBLK, jb_split, kc_split, row_count, kc_width)
    ).reshape(device_count, row_count, kc_width)
    tile_matrix = integrals[0, :, 0, :]
    partial_value = jnp.einsum(
        "srk,jk->srj",
        lax.all_to_all(outgoing, "redist", split_axis=0, concat_axis=0, tiled=True),
        tile_matrix,
        precision=lax.Precision.HIGHEST,
        preferred_element_type=jnp.float32,
    )
    moved = lax.all_to_all(partial_value, "redist", split_axis=0, concat_axis=0, tiled=True)
    arranged = arrange(moved, row_count, jb_split, kc_split, col_width, half_slots)
    result = lax.psum_scatter(arranged, "rep", scatter_dimension=2, tiled=True)
    return result * live_mask[:, None, None, :]


def solution(mesh):
    placed = (P(None, "redist", "rep", None), P("redist", None, "rep", None), P())
    return jax.shard_map(
        on_device,
        mesh=mesh,
        in_specs=placed,
        out_specs=P(None, "redist", "rep", None),
        check_vma=False,
    )
```

```python
import functools

import jax
import jax.numpy as jnp
from jax import lax
from jax.experimental import pallas as pl
from jax.experimental.pallas import tpu as pltpu
from jax.sharding import PartitionSpec as P

NBLK = 8
LANES = 128
CHUNK = 256
MESH = pl.DeviceIdType.MESH


def arrange(moved, rows, jb_split, kc_split, col_width, half_slots):
    summed = moved.reshape(NBLK, jb_split, kc_split, rows, col_width).sum(axis=2)
    return summed.transpose(0, 2, 1, 3).reshape(NBLK, rows, 2, half_slots)


def contract_and_reduce(
    amp, tiles, out, w_spill,
    a_in, a_parts, w_in, w_kept, w_stage, rep_out, rep_in, own, x_out, keep, x_in, final,
    a_send, a_recv, a_local, w_sem, w_store, w_load, rep_send, rep_recv, x_send, x_recv, o_send, o_recv, o_local,
):
    n = 2 * NBLK
    rows, half = amp.shape[1], amp.shape[2]
    width = half // 2
    pieces = width // LANES
    total = n * rows
    part = NBLK * rows
    chunks = half // CHUNK
    kept = w_kept.shape[0]
    me, core = lax.axis_index("redist"), lax.axis_index("rep")
    block, mine = me // 2, me % 2
    place = mine * NBLK + block

    def w_copy(t, slot, which):
        h = 1 - core if which == 0 else core
        first = pl.multiple_of((h * half + t * CHUNK) * pieces, 8)
        return pltpu.make_async_copy(
            tiles.at[pl.ds(first, CHUNK * pieces), :], w_in.at[slot, which], w_sem.at[slot, which]
        )

    def a_piece(tile):
        return amp.at[tile // 2, :, pl.ds(pl.multiple_of((tile % 2) * width, LANES), width)]

    def a_copy(tile):
        return pltpu.make_async_remote_copy(
            src_ref=a_piece(tile), dst_ref=a_in.at[place],
            send_sem=a_send.at[tile], recv_sem=a_recv.at[place],
            device_id=(tile, core), device_id_type=MESH,
        )

    def a_arrival(source):
        return pltpu.make_async_remote_copy(
            src_ref=a_piece(source), dst_ref=a_in.at[source % 2 * NBLK + source // 2],
            send_sem=a_send.at[source], recv_sem=a_recv.at[source % 2 * NBLK + source // 2],
            device_id=(source, core), device_id_type=MESH,
        )

    def far(i):
        return (1 - me // NBLK) * NBLK + (me + i) % NBLK

    def near(i):
        return me // NBLK * NBLK + (me + i) % NBLK

    for which in range(2):
        w_copy(0, 0, which).start()
    local = pltpu.make_async_copy(a_piece(me), a_in.at[place], a_local)
    local.start()

    barrier = pltpu.get_barrier_semaphore()
    pl.semaphore_signal(barrier, inc=1, device_id=(me, 1 - core), device_id_type=MESH)

    @pl.loop(1, n)
    def _(i):
        pl.semaphore_signal(barrier, inc=1, device_id=((me + i) % n, core), device_id_type=MESH)

    pl.semaphore_wait(barrier, n)

    @pl.loop(0, NBLK)
    def _(i):
        a_copy(far(i)).start()

    @pl.loop(1, NBLK)
    def _(i):
        a_copy(near(i)).start()

    def split(t, which, w_parts):
        w_copy(t, t % 2, which).wait()
        source = w_in.at[t % 2, which]
        for c in range(pieces):
            at = slice(c * LANES, (c + 1) * LANES)
            value = source[pl.ds(c, CHUNK, stride=pieces), :]
            high = value.astype(jnp.bfloat16)
            w_parts[:CHUNK, at] = high
            w_parts[CHUNK:, at] = (value - high.astype(jnp.float32)).astype(jnp.bfloat16)

    def fetch(t):
        @pl.when(t < chunks)
        def _():
            w_copy(t, t % 2, 0).start()
            w_copy(t, t % 2, 1).start()

    def store(t, which):
        return pltpu.make_async_copy(
            w_stage.at[t % 2, which], w_spill.at[t - kept, which], w_store.at[t % 2, which]
        )

    def load(t, which):
        return pltpu.make_async_copy(
            w_spill.at[t - kept, which], w_stage.at[t % 2, which], w_load.at[t % 2, which]
        )

    @pl.loop(0, kept)
    def _(t):
        fetch(t + 1)
        split(t, 0, w_kept.at[t, 0])
        split(t, 1, w_kept.at[t, 1])

    @pl.loop(kept, chunks)
    def _(t):
        fetch(t + 1)

        @pl.when(t >= kept + 2)
        def _():
            store(t - 2, 0).wait()
            store(t - 2, 1).wait()

        split(t, 0, w_stage.at[t % 2, 0])
        store(t, 0).start()
        split(t, 1, w_stage.at[t % 2, 1])
        store(t, 1).start()

    for t in (chunks - 2, chunks - 1):
        store(t, 0).wait()
        store(t, 1).wait()

    load(kept, 0).start()
    load(kept, 1).start()

    def split_rows(at):
        first = pl.multiple_of(at * rows, rows)
        value = a_in[at]
        high = value.astype(jnp.bfloat16)
        a_parts[pl.ds(first, rows), :] = high
        a_parts[pl.ds(total + first, rows), :] = (value - high.astype(jnp.float32)).astype(jnp.bfloat16)

    local.wait()
    split_rows(place)

    @pl.loop(1, NBLK)
    def _(i):
        source = near(i)
        a_arrival(source).wait_recv()
        split_rows(source % 2 * NBLK + source // 2)

    @pl.loop(0, NBLK)
    def _(i):
        source = far(i)
        a_arrival(source).wait_recv()
        split_rows(source % 2 * NBLK + source // 2)

    def rep_copy(t):
        return pltpu.make_async_remote_copy(
            src_ref=rep_out.at[t], dst_ref=rep_in.at[t],
            send_sem=rep_send.at[t], recv_sem=rep_recv.at[t],
            device_id=(me, 1 - core), device_id_type=MESH,
        )

    def x_copy(t):
        return pltpu.make_async_remote_copy(
            src_ref=x_out.at[t], dst_ref=x_in.at[t],
            send_sem=x_send.at[t], recv_sem=x_recv.at[t],
            device_id=(block * 2 + 1 - mine, core), device_id_type=MESH,
        )

    def o_dst(t):
        return out.at[block, :, pl.ds(pl.multiple_of(t * CHUNK, CHUNK), CHUNK)]

    def o_src(t, owner):
        return final.at[t, pl.ds(pl.multiple_of(owner * rows, rows), rows), :]

    def o_copy(t, owner):
        return pltpu.make_async_remote_copy(
            src_ref=o_src(t, owner), dst_ref=o_dst(t),
            send_sem=o_send.at[owner], recv_sem=o_recv.at[block],
            device_id=(owner * 2 + mine, core), device_id_type=MESH,
        )

    contract = functools.partial(
        lax.dot_general, dimension_numbers=(((1,), (1,)), ((), ())), preferred_element_type=jnp.float32
    )

    def product(w_parts):
        first = contract(a_parts[...], w_parts[:CHUNK, :])
        second = contract(a_parts[:total, :], w_parts[CHUNK:, :])
        return first[:total] + (first[total:] + second)

    def multiply(t, w_parts):
        rep_out[t] = product(w_parts.at[0])
        rep_copy(t).start()
        own[t % 2] = product(w_parts.at[1])

    def sum_cores(t):
        slot = t % 2
        there = pl.ds(pl.multiple_of((1 - mine) * part, part), part)
        here = pl.ds(pl.multiple_of(mine * part, part), part)
        x_out[t] = own[slot, there, :] + rep_in[t, there, :]
        x_copy(t).start()
        keep[t % 4] = own[slot, here, :] + rep_in[t, here, :]

    def sum_pieces(t):
        x_copy(t).wait_recv()
        final[t] = keep[t % 4] + x_in[t]

        @pl.loop(0, NBLK // 2)
        def _(i):
            o_copy(t, (1 - block // 4) * 4 + (block + i) % 4).start()

        @pl.loop(1, NBLK // 2)
        def _(i):
            o_copy(t, block // 4 * 4 + (block + i) % 4).start()

        pltpu.make_async_copy(o_src(t, block), o_dst(t), o_local).start()

    def settle(t):
        @pl.when(t >= 1)
        def _():
            rep_copy(t - 1).wait_recv()
            sum_cores(t - 1)

    def deliver(t):
        @pl.when(t >= 3)
        def _():
            sum_pieces(t - 3)

    @pl.loop(0, kept)
    def _(t):
        settle(t)
        multiply(t, w_kept.at[t])
        deliver(t)

    @pl.loop(kept, chunks)
    def _(t):
        settle(t)

        @pl.when(t + 1 < chunks)
        def _():
            load(t + 1, 0).start()
            load(t + 1, 1).start()

        load(t, 0).wait()
        load(t, 1).wait()
        multiply(t, w_stage.at[t % 2])
        deliver(t)

    rep_copy(chunks - 1).wait_recv()
    sum_cores(chunks - 1)

    @pl.loop(chunks - 3, chunks)
    def _(t):
        sum_pieces(t)

    @pl.loop(0, chunks)
    def _(t):
        rep_copy(t).wait_send()
        x_copy(t).wait_send()

    @pl.loop(1, n)
    def _(i):
        a_copy((me + i) % n).wait_send()

    pltpu.make_async_copy(out.at[block], out.at[block], o_local).wait()

    @pl.loop(1, NBLK)
    def _(i):
        owner = (block + i) % NBLK
        pltpu.make_async_remote_copy(
            src_ref=out.at[owner], dst_ref=out.at[owner],
            send_sem=o_send.at[owner], recv_sem=o_recv.at[owner],
            device_id=(owner * 2 + mine, core), device_id_type=MESH,
        ).wait()


def fused(masked, tiles):
    rows, half = masked.shape[1], masked.shape[2]
    width = half // 2
    total, part, chunks = 2 * NBLK * rows, NBLK * rows, half // CHUNK
    kept = chunks * 2 // 5
    f32, bf16, dma = jnp.float32, jnp.bfloat16, pltpu.SemaphoreType.DMA
    result, _ = pl.pallas_call(
        contract_and_reduce,
        out_shape=(
            jax.ShapeDtypeStruct(masked.shape, f32),
            jax.ShapeDtypeStruct((chunks - kept, 2, 2 * CHUNK, width), bf16),
        ),
        in_specs=[pl.BlockSpec(memory_space=pl.ANY)] * 2,
        out_specs=[pl.BlockSpec(memory_space=pl.ANY)] * 2,
        scratch_shapes=[
            pltpu.VMEM((2 * NBLK, rows, width), f32),
            pltpu.VMEM((2 * total, width), bf16),
            pltpu.VMEM((2, 2, CHUNK * width // LANES, LANES), f32),
            pltpu.VMEM((kept, 2, 2 * CHUNK, width), bf16),
            pltpu.VMEM((2, 2, 2 * CHUNK, width), bf16),
            pltpu.VMEM((chunks, total, CHUNK), f32),
            pltpu.VMEM((chunks, total, CHUNK), f32),
            pltpu.VMEM((2, total, CHUNK), f32),
            pltpu.VMEM((chunks, part, CHUNK), f32),
            pltpu.VMEM((4, part, CHUNK), f32),
            pltpu.VMEM((chunks, part, CHUNK), f32),
            pltpu.VMEM((chunks, part, CHUNK), f32),
            dma((2 * NBLK,)), dma((2 * NBLK,)), dma,
            dma((2, 2)), dma((2, 2)), dma((2, 2)),
            dma((chunks,)), dma((chunks,)),
            dma((chunks,)), dma((chunks,)),
            dma((NBLK,)), dma((NBLK,)), dma,
        ],
        compiler_params=pltpu.CompilerParams(
            collective_id=0, has_side_effects=True, vmem_limit_bytes=60 * 1024 * 1024
        ),
        cost_estimate=pl.CostEstimate(
            flops=6 * total * width * 2 * half, bytes_accessed=tiles.size * 4, transcendentals=0
        ),
    )(masked, tiles)
    return result


def on_device(amplitudes, integrals, pair_count):
    half_slots = amplitudes.shape[3]
    row_count = amplitudes.shape[1]
    col_width = integrals.shape[1]
    kc_width = integrals.shape[3]
    kc_split = half_slots // kc_width
    jb_split = 2 * half_slots // col_width
    device_count = lax.axis_size("redist")
    half_index = lax.axis_index("rep")
    slot_index = half_index * half_slots + lax.iota(jnp.int32, half_slots)
    live_mask = (slot_index[None, :] < pair_count[:, None]).astype(jnp.float32)
    masked = amplitudes[:, :, 0, :] * live_mask[:, None, :]
    if (
        jb_split == 1 and kc_split == 2 and device_count == 2 * NBLK
        and row_count % 16 == 0 and half_slots >= 5 * CHUNK and half_slots % CHUNK == 0 and kc_width % LANES == 0
    ):
        result = fused(masked, integrals.reshape(-1, LANES))
        return (result * live_mask[:, None, :])[:, :, None, :]
    pieces = masked.reshape(NBLK, row_count, kc_split, kc_width).transpose(0, 2, 1, 3)
    outgoing = jnp.broadcast_to(
        pieces[:, None], (NBLK, jb_split, kc_split, row_count, kc_width)
    ).reshape(device_count, row_count, kc_width)
    tile_matrix = integrals[0, :, 0, :]
    partial_value = jnp.einsum(
        "srk,jk->srj",
        lax.all_to_all(outgoing, "redist", split_axis=0, concat_axis=0, tiled=True),
        tile_matrix,
        precision=lax.Precision.HIGHEST,
        preferred_element_type=jnp.float32,
    )
    moved = lax.all_to_all(partial_value, "redist", split_axis=0, concat_axis=0, tiled=True)
    arranged = arrange(moved, row_count, jb_split, kc_split, col_width, half_slots)
    result = lax.psum_scatter(arranged, "rep", scatter_dimension=2, tiled=True)
    return result * live_mask[:, None, None, :]


def solution(mesh):
    placed = (P(None, "redist", "rep", None), P("redist", None, "rep", None), P())
    return jax.shard_map(
        on_device,
        mesh=mesh,
        in_specs=placed,
        out_specs=P(None, "redist", "rep", None),
        check_vma=False,
    )
```

```python
import functools

import jax
import jax.numpy as jnp
from jax import lax
from jax.experimental import pallas as pl
from jax.experimental.pallas import tpu as pltpu
from jax.sharding import PartitionSpec as P

NBLK = 8
LANES = 128
CHUNK = 256
MESH = pl.DeviceIdType.MESH


def arrange(moved, rows, jb_split, kc_split, col_width, half_slots):
    summed = moved.reshape(NBLK, jb_split, kc_split, rows, col_width).sum(axis=2)
    return summed.transpose(0, 2, 1, 3).reshape(NBLK, rows, 2, half_slots)


def contract_and_reduce(
    amp, tiles, out, w_spill,
    a_in, a_parts, w_in, w_kept, w_stage, rep_out, rep_in, own, x_out, keep, x_in, final,
    a_send, a_recv, a_local, w_sem, w_store, w_load, rep_send, rep_recv, x_send, x_recv, o_send, o_recv, o_local,
):
    n = 2 * NBLK
    rows, half = amp.shape[1], amp.shape[2]
    width = half // 2
    pieces = width // LANES
    total = n * rows
    part = NBLK * rows
    chunks = half // CHUNK
    kept = w_kept.shape[0]
    depth = a_parts.shape[1]
    me, core = lax.axis_index("redist"), lax.axis_index("rep")
    block, mine = me // 2, me % 2
    place = mine * NBLK + block

    def w_copy(t, slot, which):
        h = 1 - core if which == 0 else core
        first = pl.multiple_of((h * half + t * CHUNK) * pieces, 8)
        return pltpu.make_async_copy(
            tiles.at[pl.ds(first, CHUNK * pieces), :], w_in.at[slot, which], w_sem.at[slot, which]
        )

    def a_piece(tile):
        return amp.at[tile // 2, :, pl.ds(pl.multiple_of((tile % 2) * width, LANES), width)]

    def a_copy(tile):
        return pltpu.make_async_remote_copy(
            src_ref=a_piece(tile), dst_ref=a_in.at[place],
            send_sem=a_send.at[tile], recv_sem=a_recv.at[place],
            device_id=(tile, core), device_id_type=MESH,
        )

    def a_arrival(source):
        return pltpu.make_async_remote_copy(
            src_ref=a_piece(source), dst_ref=a_in.at[source % 2 * NBLK + source // 2],
            send_sem=a_send.at[source], recv_sem=a_recv.at[source % 2 * NBLK + source // 2],
            device_id=(source, core), device_id_type=MESH,
        )

    def far(i):
        return (1 - me // NBLK) * NBLK + (me + i) % NBLK

    def near(i):
        return me // NBLK * NBLK + (me + i) % NBLK

    for which in range(2):
        w_copy(0, 0, which).start()
    local = pltpu.make_async_copy(a_piece(me), a_in.at[place], a_local)
    local.start()

    barrier = pltpu.get_barrier_semaphore()
    pl.semaphore_signal(barrier, inc=1, device_id=(me, 1 - core), device_id_type=MESH)

    @pl.loop(1, n)
    def _(i):
        pl.semaphore_signal(barrier, inc=1, device_id=((me + i) % n, core), device_id_type=MESH)

    pl.semaphore_wait(barrier, n)

    @pl.loop(0, NBLK)
    def _(i):
        a_copy(far(i)).start()

    @pl.loop(1, NBLK)
    def _(i):
        a_copy(near(i)).start()

    def split(t, which, w_parts):
        w_copy(t, t % 2, which).wait()
        source = w_in.at[t % 2, which]
        for c in range(pieces):
            at = slice(c * LANES, (c + 1) * LANES)
            value = source[pl.ds(c, CHUNK, stride=pieces), :]
            high = value.astype(jnp.bfloat16)
            w_parts[:CHUNK, at] = high
            w_parts[CHUNK:, at] = (value - high.astype(jnp.float32)).astype(jnp.bfloat16)
        if depth > width:
            w_parts[:, width:] = jnp.zeros((2 * CHUNK, depth - width), jnp.bfloat16)

    def fetch(t):
        @pl.when(t < chunks)
        def _():
            w_copy(t, t % 2, 0).start()
            w_copy(t, t % 2, 1).start()

    def store(t, which):
        return pltpu.make_async_copy(
            w_stage.at[t % 2, which, :, pl.ds(0, width)], w_spill.at[t - kept, which], w_store.at[t % 2, which]
        )

    def load(t, which):
        return pltpu.make_async_copy(
            w_spill.at[t - kept, which], w_stage.at[t % 2, which, :, pl.ds(0, width)], w_load.at[t % 2, which]
        )

    @pl.loop(0, kept)
    def _(t):
        fetch(t + 1)
        split(t, 0, w_kept.at[t, 0])
        split(t, 1, w_kept.at[t, 1])

    @pl.loop(kept, chunks)
    def _(t):
        fetch(t + 1)

        @pl.when(t >= kept + 2)
        def _():
            store(t - 2, 0).wait()
            store(t - 2, 1).wait()

        split(t, 0, w_stage.at[t % 2, 0])
        store(t, 0).start()
        split(t, 1, w_stage.at[t % 2, 1])
        store(t, 1).start()

    for t in (chunks - 2, chunks - 1):
        store(t, 0).wait()
        store(t, 1).wait()

    load(kept, 0).start()
    load(kept, 1).start()

    def split_rows(at):
        first = pl.multiple_of(at * rows, rows)
        value = a_in[at]
        high = value.astype(jnp.bfloat16)
        a_parts[pl.ds(first, rows), :width] = high
        a_parts[pl.ds(total + first, rows), :width] = (value - high.astype(jnp.float32)).astype(jnp.bfloat16)

    if depth > width:
        a_parts[:, width:] = jnp.zeros((2 * total, depth - width), jnp.bfloat16)
    local.wait()
    split_rows(place)

    @pl.loop(1, NBLK)
    def _(i):
        source = near(i)
        a_arrival(source).wait_recv()
        split_rows(source % 2 * NBLK + source // 2)

    @pl.loop(0, NBLK)
    def _(i):
        source = far(i)
        a_arrival(source).wait_recv()
        split_rows(source % 2 * NBLK + source // 2)

    def rep_copy(t):
        return pltpu.make_async_remote_copy(
            src_ref=rep_out.at[t], dst_ref=rep_in.at[t],
            send_sem=rep_send.at[t], recv_sem=rep_recv.at[t],
            device_id=(me, 1 - core), device_id_type=MESH,
        )

    def x_copy(t):
        return pltpu.make_async_remote_copy(
            src_ref=x_out.at[t], dst_ref=x_in.at[t],
            send_sem=x_send.at[t], recv_sem=x_recv.at[t],
            device_id=(block * 2 + 1 - mine, core), device_id_type=MESH,
        )

    def o_dst(t):
        return out.at[block, :, pl.ds(pl.multiple_of(t * CHUNK, CHUNK), CHUNK)]

    def o_src(t, owner):
        return final.at[t, pl.ds(pl.multiple_of(owner * rows, rows), rows), :]

    def o_copy(t, owner):
        return pltpu.make_async_remote_copy(
            src_ref=o_src(t, owner), dst_ref=o_dst(t),
            send_sem=o_send.at[owner], recv_sem=o_recv.at[block],
            device_id=(owner * 2 + mine, core), device_id_type=MESH,
        )

    contract = functools.partial(
        lax.dot_general, dimension_numbers=(((1,), (1,)), ((), ())), preferred_element_type=jnp.float32
    )

    def product(w_parts):
        first = contract(a_parts[...], w_parts[:CHUNK, :])
        second = contract(a_parts[:total, :], w_parts[CHUNK:, :])
        return first[:total] + (first[total:] + second)

    def multiply(t, w_parts):
        rep_out[t] = product(w_parts.at[0])
        rep_copy(t).start()
        deliver(t)
        own[t % 2] = product(w_parts.at[1])

    def sum_cores(t):
        slot = t % 2
        there = pl.ds(pl.multiple_of((1 - mine) * part, part), part)
        here = pl.ds(pl.multiple_of(mine * part, part), part)
        x_out[t] = own[slot, there, :] + rep_in[t, there, :]
        x_copy(t).start()
        keep[t % 4] = own[slot, here, :] + rep_in[t, here, :]

    def sum_pieces(t):
        x_copy(t).wait_recv()
        final[t] = keep[t % 4] + x_in[t]

        @pl.loop(0, NBLK // 2)
        def _(i):
            o_copy(t, (1 - block // 4) * 4 + (block + i) % 4).start()

        @pl.loop(1, NBLK // 2)
        def _(i):
            o_copy(t, block // 4 * 4 + (block + i) % 4).start()

        pltpu.make_async_copy(o_src(t, block), o_dst(t), o_local).start()

    def settle(t):
        @pl.when(t >= 1)
        def _():
            rep_copy(t - 1).wait_recv()
            sum_cores(t - 1)

    def deliver(t):
        @pl.when(t >= 2)
        def _():
            sum_pieces(t - 2)

    @pl.loop(0, kept)
    def _(t):
        settle(t)
        multiply(t, w_kept.at[t])

    @pl.loop(kept, chunks)
    def _(t):
        settle(t)

        @pl.when(t + 1 < chunks)
        def _():
            load(t + 1, 0).start()
            load(t + 1, 1).start()

        load(t, 0).wait()
        load(t, 1).wait()
        multiply(t, w_stage.at[t % 2])

    rep_copy(chunks - 1).wait_recv()
    sum_cores(chunks - 1)

    @pl.loop(chunks - 2, chunks)
    def _(t):
        sum_pieces(t)

    @pl.loop(0, chunks)
    def _(t):
        rep_copy(t).wait_send()
        x_copy(t).wait_send()

    @pl.loop(1, n)
    def _(i):
        a_copy((me + i) % n).wait_send()

    pltpu.make_async_copy(out.at[block], out.at[block], o_local).wait()

    @pl.loop(1, NBLK)
    def _(i):
        owner = (block + i) % NBLK
        pltpu.make_async_remote_copy(
            src_ref=out.at[owner], dst_ref=out.at[owner],
            send_sem=o_send.at[owner], recv_sem=o_recv.at[owner],
            device_id=(owner * 2 + mine, core), device_id_type=MESH,
        ).wait()


def fused(masked, tiles):
    rows, half = masked.shape[1], masked.shape[2]
    width = half // 2
    total, part, chunks = 2 * NBLK * rows, NBLK * rows, half // CHUNK
    kept = chunks // 3
    depth = (width + CHUNK - 1) // CHUNK * CHUNK
    f32, bf16, dma = jnp.float32, jnp.bfloat16, pltpu.SemaphoreType.DMA
    result, _ = pl.pallas_call(
        contract_and_reduce,
        out_shape=(
            jax.ShapeDtypeStruct(masked.shape, f32),
            jax.ShapeDtypeStruct((chunks - kept, 2, 2 * CHUNK, width), bf16),
        ),
        in_specs=[pl.BlockSpec(memory_space=pl.ANY)] * 2,
        out_specs=[pl.BlockSpec(memory_space=pl.ANY)] * 2,
        scratch_shapes=[
            pltpu.VMEM((2 * NBLK, rows, width), f32),
            pltpu.VMEM((2 * total, depth), bf16),
            pltpu.VMEM((2, 2, CHUNK * width // LANES, LANES), f32),
            pltpu.VMEM((kept, 2, 2 * CHUNK, depth), bf16),
            pltpu.VMEM((2, 2, 2 * CHUNK, depth), bf16),
            pltpu.VMEM((chunks, total, CHUNK), f32),
            pltpu.VMEM((chunks, total, CHUNK), f32),
            pltpu.VMEM((2, total, CHUNK), f32),
            pltpu.VMEM((chunks, part, CHUNK), f32),
            pltpu.VMEM((4, part, CHUNK), f32),
            pltpu.VMEM((chunks, part, CHUNK), f32),
            pltpu.VMEM((chunks, part, CHUNK), f32),
            dma((2 * NBLK,)), dma((2 * NBLK,)), dma,
            dma((2, 2)), dma((2, 2)), dma((2, 2)),
            dma((chunks,)), dma((chunks,)),
            dma((chunks,)), dma((chunks,)),
            dma((NBLK,)), dma((NBLK,)), dma,
        ],
        compiler_params=pltpu.CompilerParams(
            collective_id=0, has_side_effects=True, vmem_limit_bytes=60 * 1024 * 1024
        ),
        cost_estimate=pl.CostEstimate(
            flops=6 * total * width * 2 * half, bytes_accessed=tiles.size * 4, transcendentals=0
        ),
    )(masked, tiles)
    return result


def on_device(amplitudes, integrals, pair_count):
    half_slots = amplitudes.shape[3]
    row_count = amplitudes.shape[1]
    col_width = integrals.shape[1]
    kc_width = integrals.shape[3]
    kc_split = half_slots // kc_width
    jb_split = 2 * half_slots // col_width
    device_count = lax.axis_size("redist")
    half_index = lax.axis_index("rep")
    slot_index = half_index * half_slots + lax.iota(jnp.int32, half_slots)
    live_mask = (slot_index[None, :] < pair_count[:, None]).astype(jnp.float32)
    masked = amplitudes[:, :, 0, :] * live_mask[:, None, :]
    if (
        jb_split == 1 and kc_split == 2 and device_count == 2 * NBLK
        and row_count % 16 == 0 and half_slots >= 5 * CHUNK and half_slots % CHUNK == 0 and kc_width % LANES == 0
    ):
        result = fused(masked, integrals.reshape(-1, LANES))
        return (result * live_mask[:, None, :])[:, :, None, :]
    pieces = masked.reshape(NBLK, row_count, kc_split, kc_width).transpose(0, 2, 1, 3)
    outgoing = jnp.broadcast_to(
        pieces[:, None], (NBLK, jb_split, kc_split, row_count, kc_width)
    ).reshape(device_count, row_count, kc_width)
    tile_matrix = integrals[0, :, 0, :]
    partial_value = jnp.einsum(
        "srk,jk->srj",
        lax.all_to_all(outgoing, "redist", split_axis=0, concat_axis=0, tiled=True),
        tile_matrix,
        precision=lax.Precision.HIGHEST,
        preferred_element_type=jnp.float32,
    )
    moved = lax.all_to_all(partial_value, "redist", split_axis=0, concat_axis=0, tiled=True)
    arranged = arrange(moved, row_count, jb_split, kc_split, col_width, half_slots)
    result = lax.psum_scatter(arranged, "rep", scatter_dimension=2, tiled=True)
    return result * live_mask[:, None, None, :]


def solution(mesh):
    placed = (P(None, "redist", "rep", None), P("redist", None, "rep", None), P())
    return jax.shard_map(
        on_device,
        mesh=mesh,
        in_specs=placed,
        out_specs=P(None, "redist", "rep", None),
        check_vma=False,
    )
```
